256 devices in a mesh: tm: 8 (over z), tile: 32 (over x, y, core).
Axes of the slice: x: 4, y: 4, z: 8, core: 2. Of those that a mesh axis runs over, the one named last changes fastest.
Arguments:
- latents: bfloat16 [32, 16, 16, 256], P('tile', 'tm'), may hold values from -6 to 6
- writer: int32 [32], replicated, may hold values from 0 to 31, as said below
- margin_cols: int32 [32], P('tile'), may hold values from 0 to 4, as said below
- in_weight: bfloat16 [3, 144, 512], replicated, may hold values from -0.3125 to 0.3125
- in_bias: float32 [512], replicated, may hold values from -3 to 3
- mid_weight: bfloat16 [3, 4608, 256], replicated, may hold values from -0.0546875 to 0.0546875
- mid_bias: float32 [256], replicated, may hold values from -3 to 3
- skip_weight: bfloat16 [512, 256], replicated, may hold values from -0.25 to 0.25
- head_weight: bfloat16 [256, 3], replicated, may hold values from -0.375 to 0.375
- head_bias: float32 [3], replicated, may hold values from -3 to 3
Outputs:
- written: bfloat16 [96, 16, 3, 256], P('tile', 'tm')
- blended: bfloat16 [32, 16, 3, 256], P('tile', 'tm')
The draws below stay inside these ranges and needn't reach their ends.
Inputs may be any that keep to these rules, and one draw needn't show every extreme that they name: `writer`: each device of tile is named at most 3 times, and one device exactly 3 times. `margin_cols`: 0 where a tile starts a clip, always for tile 0; otherwise from 2 to 4.
All inputs are finite; a program needn't handle non-finite values.
Results may differ from the reference program's by a relative error of at most 0.015.
Values may be sent and summed in bfloat16 or wider, within the bound.
A program may use at most 128 MiB of HBM per device.

```python
import jax
import jax.numpy as jnp
from jax import lax

C_LAT = 16
C_MID = 512
C_OUT = 256
TH = 16
TW = 16
PIX = 256
FRAMES = 16
MAXLOAD = 3
TILES = 32
WSLOTS = 96
MARGIN_LO = 2
MARGIN_HI = 4


def draw_writer(key, part):
    key = jax.random.fold_in(key, 7)
    key_busy, key_order, key_tiles = jax.random.split(key, 3)
    busiest = jax.random.randint(key_busy, (), 0, WSLOTS // MAXLOAD)
    slot_ids = jnp.arange(WSLOTS, dtype=jnp.int32)
    scores = jax.random.permutation(key_order, WSLOTS).astype(jnp.int32)
    scores = jnp.where(slot_ids // MAXLOAD == busiest, slot_ids % MAXLOAD - MAXLOAD, scores)
    chosen = jnp.argsort(scores, stable=True)[:TILES]
    order_perm = jax.random.permutation(key_tiles, TILES)
    return (chosen[order_perm] // MAXLOAD).astype(jnp.int32)


def draw_margin_cols(key, part):
    key = jax.random.fold_in(key, 11)
    key_width, key_start, key_pin = jax.random.split(key, 3)
    widths = jax.random.randint(key_width, (TILES,), MARGIN_LO, MARGIN_HI + 1)
    starts = jax.random.randint(key_start, (TILES,), 0, 4) == 0
    pinned = jax.random.randint(key_pin, (), 1, TILES)
    positions = jnp.arange(TILES, dtype=jnp.int32)
    widths = jnp.where(starts, 0, widths)
    widths = jnp.where(positions == 0, 0, widths)
    widths = jnp.where(positions == pinned, MARGIN_HI, widths)
    return widths.astype(jnp.int32)


def steps_of(stream_key, dims, cuts, low, largest):
    gain = 1.0
    for dim, parts in cuts:
        heights = jax.random.uniform(jax.random.fold_in(jax.random.fold_in(stream_key, 6), dim), (parts,), jnp.float32, low / len(cuts), largest / len(cuts))
        gain = gain * jnp.repeat(jnp.exp(heights), dims[dim] // parts).reshape((-1,) + (1,) * (len(dims) - 1 - dim))
    return gain


def normal_values(key, dims, spread, reach, cuts=(), kind=jnp.bfloat16):
    factor_of = steps_of(key, dims, cuts, -0.22, 0.18) if cuts else 1.0
    result = jax.random.normal(key, dims, jnp.float32) * spread * factor_of
    return jnp.minimum(jnp.maximum(result, -reach), reach).astype(kind)


def setup_inputs(seed: int = 0) -> dict:
    arg_keys = jax.random.split(jax.random.key(seed), 11)
    return {
        "latents": normal_values(arg_keys[0], (TILES, FRAMES, C_LAT, PIX), 1.0, 6.0, ((0, 32), (1, 8))),
        "writer": draw_writer(jax.random.fold_in(arg_keys[10], 71), 0),
        "margin_cols": draw_margin_cols(jax.random.fold_in(arg_keys[10], 71), 0),
        "in_weight": normal_values(arg_keys[3], (3, 9 * C_LAT, C_MID), (27 * C_LAT) ** -0.5, 0.3125),
        "in_bias": normal_values(arg_keys[4], (C_MID,), 0.5, 3.0, (), jnp.float32),
        "mid_weight": normal_values(arg_keys[5], (3, 9 * C_MID, C_OUT), (27 * C_MID) ** -0.5, 0.0546875),
        "mid_bias": normal_values(arg_keys[6], (C_OUT,), 0.5, 3.0, (), jnp.float32),
        "skip_weight": normal_values(arg_keys[7], (C_MID, C_OUT), C_MID ** -0.5, 0.25),
        "head_weight": normal_values(arg_keys[8], (C_OUT, 3), C_OUT ** -0.5, 0.375),
        "head_bias": normal_values(arg_keys[9], (3,), 0.5, 3.0, (), jnp.float32),
    }


def spread_taps(values):
    frame_count, channels, _ = values.shape
    tile_grid = values.reshape(frame_count, channels, TH, TW)
    padded = jnp.pad(tile_grid, ((0, 0), (0, 0), (1, 1), (1, 1)), mode="edge")
    pieces = []
    for row_step in range(3):
        for col_step in range(3):
            window = padded[:, :, row_step:row_step + TH, col_step:col_step + TW]
            pieces.append(window.reshape(frame_count, channels, TH * TW))
    return jnp.concatenate(pieces, axis=1)


def causal_conv(values, weight, offset):
    columns = spread_taps(values).astype(jnp.float32)
    steps_out = values.shape[0] - 2
    summed = jnp.zeros((steps_out, weight.shape[2], values.shape[2]), jnp.float32)
    for time_lag in range(3):
        summed = summed + jnp.einsum("fkp,ko->fop", columns[time_lag:time_lag + steps_out], weight[time_lag].astype(jnp.float32))
    return summed + offset[:, None]


def decode_tile(latent, in_weight, in_bias, mid_weight, mid_bias, skip_weight, head_weight, head_bias):
    padded_in = jnp.concatenate([latent[:1], latent[:1], latent], axis=0)
    first_out = causal_conv(padded_in, in_weight, in_bias).astype(jnp.bfloat16)
    active = jax.nn.silu(first_out.astype(jnp.float32)).astype(jnp.bfloat16)
    active = jnp.concatenate([active[:1], active[:1], active], axis=0)
    middle = causal_conv(active, mid_weight, mid_bias)
    middle = middle + jnp.einsum("fcp,co->fop", first_out.astype(jnp.float32), skip_weight.astype(jnp.float32))
    gated_mid = jax.nn.silu(middle).astype(jnp.bfloat16)
    pixels = jnp.einsum("fcp,co->fop", gated_mid.astype(jnp.float32), head_weight.astype(jnp.float32)) + head_bias[:, None]
    return pixels.astype(jnp.bfloat16)


def blend_tiles(decoded, margin_cols):
    tile_count = decoded.shape[0]
    current = decoded.astype(jnp.float32).reshape(tile_count, FRAMES, 3, TH, TW)
    before = jnp.concatenate([current[:1], current[:-1]], axis=0)
    columns = jnp.arange(TW, dtype=jnp.int32)
    widths = margin_cols[:, None]
    inside = columns[None, :] < widths
    source = jnp.clip(TW - widths + columns[None, :], 0, TW - 1)
    chooser = (columns[None, None, :] == source[:, :, None]).astype(jnp.float32)
    prev_cols = jnp.einsum("tfcry,txy->tfcrx", before, chooser)
    fraction = columns[None, :].astype(jnp.float32) / jnp.maximum(widths, 1).astype(jnp.float32)
    weight_new = jnp.where(inside, fraction, 1.0)
    weight_old = jnp.where(inside, 1.0 - fraction, 0.0)
    blended = current * weight_new[:, None, None, None, :] + prev_cols * weight_old[:, None, None, None, :]
    return blended.astype(jnp.bfloat16).reshape(tile_count, FRAMES, 3, TH * TW)


def reference(latents, writer, margin_cols, in_weight, in_bias, mid_weight, mid_bias, skip_weight, head_weight, head_bias):
    decoded = lax.map(lambda latent: decode_tile(latent, in_weight, in_bias, mid_weight, mid_bias, skip_weight, head_weight, head_bias), latents)
    tile_ids = jnp.arange(TILES, dtype=jnp.int32)
    earlier = (writer[None, :] == writer[:, None]) & (tile_ids[None, :] < tile_ids[:, None])
    slot_rank = jnp.sum(earlier.astype(jnp.int32), axis=1).astype(jnp.int32)
    slot_of = (writer * MAXLOAD + slot_rank).astype(jnp.int32)
    written = jnp.zeros((WSLOTS, FRAMES, 3, TH * TW), jnp.bfloat16).at[slot_of].set(decoded)
    blended = blend_tiles(decoded, margin_cols)
    return (written, blended)
```

```python
import jax
import jax.numpy as jnp
from jax import lax
from jax.experimental import pallas as pl
from jax.experimental.pallas import tpu as pltpu
from jax.sharding import PartitionSpec as P

TH = 16
TW = 16
PIX = TH * TW
C_LAT = 16
C_MID = 512
C_OUT = 256
TAPS = 9 * C_LAT
MAXLOAD = 3
MARGIN_LO = 2
MARGIN_HI = 4
MESH = pl.DeviceIdType.MESH
F32 = jnp.float32
BF16 = jnp.bfloat16


def silu(v):
    return 0.5 * v * (1.0 + jnp.tanh(0.5 * v))


def remote(src, dst, send_sem, recv_sem, tm, tile):
    return pltpu.make_async_remote_copy(
        src_ref=src,
        dst_ref=dst,
        send_sem=send_sem,
        recv_sem=recv_sem,
        device_id=(tm, tile),
        device_id_type=MESH,
    )


def spread_columns(cols, lat, first, count):
    lane = lax.broadcasted_iota(jnp.int32, (count * C_LAT, PIX), 1)
    in_row = lane % TW
    x = lat[first : first + count].astype(F32).reshape(count * C_LAT, PIX)
    up = jnp.where(lane < TW, x, pltpu.roll(x, TW, 1))
    down = jnp.where(lane >= PIX - TW, x, pltpu.roll(x, PIX - TW, 1))
    for a, v in enumerate((up, x, down)):
        left = jnp.where(in_row == 0, v, pltpu.roll(v, 1, 1))
        right = jnp.where(in_row == TW - 1, v, pltpu.roll(v, PIX - 1, 1))
        for e, s in enumerate((left, v, right)):
            s = s.astype(BF16)
            for k in range(count):
                at = (first + k) * TAPS + (3 * a + e) * C_LAT
                cols[at : at + C_LAT, :] = s[k * C_LAT : (k + 1) * C_LAT]


def shift_rows(z, in_row, step):
    if step < 0:
        return jnp.where(in_row == 0, z, pltpu.roll(z, 1, 0))
    return jnp.where(in_row == TW - 1, z, pltpu.roll(z, PIX - 1, 0))


def decode_kernel(
    tiles,
    groups,
    lat_in,
    writer_in,
    margin_in,
    in_w_in,
    in_b_in,
    mid_w_in,
    mid_b_in,
    skip_w_in,
    head_w_in,
    head_b_in,
    written_out,
    blended_out,
    lat,
    cols,
    w_in,
    b_in,
    w_mid,
    b_mid,
    w_skip,
    w_head,
    u,
    v,
    first_out,
    acc,
    gated,
    gather,
    written,
    blended,
    s_writer,
    s_margin,
    s_head_b,
    halo_send,
    halo_recv,
    all_send,
    all_recv,
    load_sem,
    chunk_sem,
    out_sem,
):
    tm = lax.axis_index("tm")
    tile = lax.axis_index("tile")

    barrier = pltpu.get_barrier_semaphore()
    for d in (1, 2):

        @pl.when(tm >= d)
        def _():
            pl.semaphore_signal(barrier, inc=1, device_id=(tm - d, tile), device_id_type=MESH)

    own = pltpu.make_async_copy(lat_in.at[0], lat.at[4:6], load_sem.at[0])
    own.start()
    loads = []
    for k, (src, dst) in enumerate(
        (
            (in_w_in, w_in),
            (in_b_in, b_in),
            (head_w_in, w_head),
            (mid_b_in, b_mid),
            (writer_in, s_writer),
            (margin_in, s_margin),
            (head_b_in, s_head_b),
            (skip_w_in, w_skip),
        )
    ):
        copy = pltpu.make_async_copy(src, dst, load_sem.at[k + 1])
        copy.start()
        loads.append(copy)
    chunks = []
    for k in range(9):
        rows = slice(k * C_MID, (k + 1) * C_MID)
        copy = pltpu.make_async_copy(mid_w_in.at[:, rows], w_mid.at[:, rows], chunk_sem.at[k])
        copy.start()
        chunks.append(copy)
    for i in range(1, tiles):
        pl.semaphore_signal(
            barrier, inc=1, device_id=(tm, lax.rem(tile + i, tiles)), device_id_type=MESH
        )
    expected = (
        tiles - 1 + (tm < groups - 1).astype(jnp.int32) + (tm < groups - 2).astype(jnp.int32)
    )
    pl.semaphore_wait(barrier, expected)

    def halo(d):
        return remote(
            lat_in.at[0],
            lat.at[4 - 2 * d : 6 - 2 * d],
            halo_send.at[d - 1],
            halo_recv.at[d - 1],
            tm + d if d > 0 else tm,
            tile,
        )

    for d in (1, 2):

        @pl.when(tm < groups - d)
        def _():
            halo(d).start()

    own.wait()
    spread_columns(cols, lat, 4, 2)

    for k in range(9):
        chunks[k].wait()

        @pl.loop(0, C_MID // 64)
        def _(s):
            rows = pl.ds(pl.multiple_of(k * C_MID + s * 64, 64), 64)
            even = w_mid[0, rows, :].astype(F32) + w_mid[2, rows, :].astype(F32)
            odd = w_mid[1, rows, :].astype(F32)
            u[0, rows, :] = (even + odd).astype(BF16)
            u[1, rows, :] = (even - odd).astype(BF16)

    for copy in loads:
        copy.wait()

    for d in (1, 2):

        @pl.when(tm >= d)
        def _():
            halo(d).wait_recv()

    @pl.when(tm == 0)
    def _():
        for g in range(4):
            lat[g] = lat[4]

    @pl.when(tm == 1)
    def _():
        for g in range(2):
            lat[g] = lat[2]

    spread_columns(cols, lat, 0, 4)

    weight = w_in[...].reshape(3 * TAPS, C_MID)
    acts = []
    for j in range(4):
        out = lax.dot_general(
            cols[j * TAPS : (j + 3) * TAPS, :],
            weight,
            (((0,), (0,)), ((), ())),
            preferred_element_type=F32,
        )
        out = (out + b_in[...]).astype(BF16)
        if j >= 2:
            first_out[j - 2] = out
        acts.append(silu(out.astype(F32)))
        if j == 2:
            mixed = (
                (0, acts[0] - acts[2]),
                (1, 0.5 * (acts[1] + acts[2])),
                (2, 0.5 * (acts[2] - acts[1])),
            )
        elif j == 3:
            mixed = ((3, acts[1] - acts[3]),)
        else:
            mixed = ()
        for i, m in mixed:
            m = m.astype(BF16)
            v[i, TW : TW + PIX, :] = m
            v[i, 0:TW, :] = m[0:TW]
            v[i, TW + PIX : 2 * TW + PIX, :] = m[PIX - TW : PIX]

    in_row = lax.broadcasted_iota(jnp.int32, (PIX, C_OUT), 0) % TW

    def product(i, e):
        frames, weights = [], []
        for r in range(3):
            rows = slice((3 * r + e) * C_MID, (3 * r + e + 1) * C_MID)
            frames.append(v[i, TW * r : TW * r + PIX, :])
            if i in (0, 3):
                weights.append(w_mid[0 if i == 0 else 2, rows, :])
            else:
                weights.append(u[i - 1, rows, :])
        return jnp.dot(
            jnp.concatenate(frames, axis=1),
            jnp.concatenate(weights, axis=0),
            preferred_element_type=F32,
        )

    def finish(f, sums):
        total = sums[1] + shift_rows(sums[0], in_row, -1) + shift_rows(sums[2], in_row, 1)
        total = total + jnp.dot(first_out[f], w_skip[...], preferred_element_type=F32) + b_mid[...]
        gated[:, f * C_OUT : (f + 1) * C_OUT] = silu(total).astype(BF16)

    for e in range(3):
        p1 = product(1, e)
        acc[0, e] = p1
        acc[1, e] = p1
    for e in range(3):
        p2 = product(2, e)
        acc[0, e] += p2
        acc[1, e] -= p2
    finish(0, [acc[0, e] + product(0, e) for e in range(3)])
    finish(1, [acc[1, e] - product(3, e) for e in range(3)])

    row = lax.broadcasted_iota(jnp.int32, (8, C_OUT), 0)
    head = w_head[...].astype(F32)
    by_color = jnp.where(
        row // 2 == 0,
        head[0:1],
        jnp.where(row // 2 == 1, head[1:2], jnp.where(row // 2 == 2, head[2:3], 0.0)),
    )
    head2 = jnp.concatenate(
        [jnp.where(row % 2 == 0, by_color, 0.0), jnp.where(row % 2 == 1, by_color, 0.0)], axis=1
    ).astype(BF16)
    pixels = lax.dot_general(
        head2, gated[...], (((1,), (1,)), ((), ())), preferred_element_type=F32
    )
    pixels = pixels + jnp.where(
        row // 2 == 0, s_head_b[0], jnp.where(row // 2 == 1, s_head_b[1], s_head_b[2])
    )
    gather[tile] = jnp.concatenate([pixels[:, :128], pixels[:, 128:]], axis=0).astype(BF16)

    for i in range(1, tiles):
        to = lax.rem(tile + i, tiles)
        remote(gather.at[tile], gather.at[tile], all_send, all_recv, tm, to).start()
    everyone = remote(
        gather.at[0 : tiles - 1],
        gather.at[0 : tiles - 1],
        all_send,
        all_recv,
        tm,
        lax.rem(tile + 1, tiles),
    )

    found = jnp.int32(0)
    which = [jnp.int32(0)] * MAXLOAD
    taken = [jnp.int32(0)] * MAXLOAD
    for t in range(tiles):
        mine = s_writer[t] == tile
        for j in range(MAXLOAD):
            hit = jnp.logical_and(mine, found == j)
            which[j] = jnp.where(hit, t, which[j])
            taken[j] = jnp.where(hit, 1, taken[j])
        found = found + mine.astype(jnp.int32)

    everyone.wait_recv()

    def tile_pixels(t):
        block = gather[t].astype(F32)
        return jnp.concatenate([block[0:8], block[8:16]], axis=1)

    for j in range(MAXLOAD):
        live = jnp.full((8, PIX), taken[j], jnp.int32) > 0
        block = jnp.where(live, tile_pixels(which[j]), 0.0).astype(BF16)
        for c in range(3):
            written[j, c] = block[2 * c : 2 * c + 2]
    margin = s_margin[0]
    width = jnp.full((8, PIX), margin, jnp.int32)
    column = lax.broadcasted_iota(jnp.int32, (8, PIX), 1) % TW
    current = tile_pixels(tile)
    before = tile_pixels(jnp.maximum(tile - 1, 0))
    prior = pltpu.roll(before, PIX - TW + MARGIN_LO, 1)
    for m in range(MARGIN_LO + 1, MARGIN_HI + 1):
        prior = jnp.where(width == m, pltpu.roll(before, PIX - TW + m, 1), prior)
    fraction = column.astype(F32) / jnp.maximum(width, 1).astype(F32)
    mix = jnp.where(column < width, (1.0 - fraction) * prior + fraction * current, current)
    mix = mix.astype(BF16)
    for c in range(3):
        blended[0, c] = mix[2 * c : 2 * c + 2]
    outs = [
        pltpu.make_async_copy(written, written_out, out_sem.at[0]),
        pltpu.make_async_copy(blended, blended_out, out_sem.at[1]),
    ]
    for copy in outs:
        copy.start()
    everyone.wait_send()
    for d in (1, 2):

        @pl.when(tm < groups - d)
        def _():
            halo(d).wait_send()

    for copy in outs:
        copy.wait()


def copy_kernel(written_in, blended_in, written_out, blended_out, sem):
    copies = [
        pltpu.make_async_copy(written_in, written_out, sem.at[0]),
        pltpu.make_async_copy(blended_in, blended_out, sem.at[1]),
    ]
    for copy in copies:
        copy.start()
    for copy in copies:
        copy.wait()


def per_device(
    latents,
    writer,
    margin_cols,
    in_weight,
    in_bias,
    mid_weight,
    mid_bias,
    skip_weight,
    head_weight,
    head_bias,
):
    tiles = lax.axis_size("tile")
    groups = lax.axis_size("tm")
    frames = latents.shape[1]
    shapes = (
        jax.ShapeDtypeStruct((MAXLOAD, 3, frames, PIX), BF16),
        jax.ShapeDtypeStruct((1, 3, frames, PIX), BF16),
    )
    anywhere = pl.BlockSpec(memory_space=pl.ANY)

    def body(*refs):
        decode_kernel(tiles, groups, *refs)

    written, blended = pl.pallas_call(
        body,
        out_shape=shapes,
        in_specs=[anywhere] * 10,
        out_specs=(anywhere,) * 2,
        scratch_shapes=[
            pltpu.VMEM((6, C_LAT, PIX), BF16),
            pltpu.VMEM((6 * TAPS, PIX), BF16),
            pltpu.VMEM((3, TAPS, C_MID), BF16),
            pltpu.VMEM((1, C_MID), F32),
            pltpu.VMEM((3, 9 * C_MID, C_OUT), BF16),
            pltpu.VMEM((1, C_OUT), F32),
            pltpu.VMEM((C_MID, C_OUT), BF16),
            pltpu.VMEM((3, C_OUT), BF16),
            pltpu.VMEM((2, 9 * C_MID, C_OUT), BF16),
            pltpu.VMEM((4, PIX + 2 * TW, C_MID), BF16),
            pltpu.VMEM((2, PIX, C_MID), BF16),
            pltpu.VMEM((2, 3, PIX, C_OUT), F32),
            pltpu.VMEM((PIX, 2 * C_OUT), BF16),
            pltpu.VMEM((tiles, 16, 128), BF16),
            pltpu.VMEM((MAXLOAD, 3, frames, PIX), BF16),
            pltpu.VMEM((1, 3, frames, PIX), BF16),
            pltpu.SMEM((tiles,), jnp.int32),
            pltpu.SMEM((1,), jnp.int32),
            pltpu.SMEM((3,), F32),
            pltpu.SemaphoreType.DMA((2,)),
            pltpu.SemaphoreType.DMA((2,)),
            pltpu.SemaphoreType.DMA,
            pltpu.SemaphoreType.DMA,
            pltpu.SemaphoreType.DMA((9,)),
            pltpu.SemaphoreType.DMA((9,)),
            pltpu.SemaphoreType.DMA((2,)),
        ],
        compiler_params=pltpu.CompilerParams(
            collective_id=0, has_side_effects=True, vmem_limit_bytes=60 * 2**20
        ),
        name="decode",
    )(
        latents,
        writer,
        margin_cols,
        in_weight,
        in_bias.reshape(1, -1),
        mid_weight,
        mid_bias.reshape(1, -1),
        skip_weight,
        head_weight.T,
        head_bias,
    )
    written, blended = pl.pallas_call(
        copy_kernel,
        out_shape=shapes,
        in_specs=[anywhere] * 2,
        out_specs=(anywhere,) * 2,
        scratch_shapes=[pltpu.SemaphoreType.DMA((2,))],
        name="hand_out",
    )(written, blended)
    return written.transpose(0, 2, 1, 3), blended.transpose(0, 2, 1, 3)


def solution(mesh):
    return jax.shard_map(
        per_device,
        mesh=mesh,
        in_specs=(P("tile", "tm", None, None), P(), P("tile"), P(), P(), P(), P(), P(), P(), P()),
        out_specs=(P("tile", "tm", None, None), P("tile", "tm", None, None)),
        check_vma=False,
    )
```

```python
import jax
import jax.numpy as jnp
from jax import lax
from jax.experimental import pallas as pl
from jax.experimental.pallas import tpu as pltpu
from jax.sharding import PartitionSpec as P

TH = 16
TW = 16
PIX = TH * TW
C_LAT = 16
C_MID = 512
C_OUT = 256
TAPS = 9 * C_LAT
MAXLOAD = 3
MARGIN_LO = 2
MARGIN_HI = 4
SIDE = 4
CORES = 2
MESH = pl.DeviceIdType.MESH
RELAYED = 3
FAR_FIRST = sorted(
    (
        (dx, dy, dc)
        for dx in range(SIDE)
        for dy in range(SIDE)
        for dc in range(CORES)
        if dx or dy or dc
    ),
    key=lambda p: -min(p[0], SIDE - p[0]) - min(p[1], SIDE - p[1]),
)
F32 = jnp.float32
BF16 = jnp.bfloat16


def silu(v):
    return 0.5 * v * (1.0 + jnp.tanh(0.5 * v))


def remote(src, dst, send_sem, recv_sem, tm, tile):
    return pltpu.make_async_remote_copy(
        src_ref=src,
        dst_ref=dst,
        send_sem=send_sem,
        recv_sem=recv_sem,
        device_id=(tm, tile),
        device_id_type=MESH,
    )


def spread_columns(cols, lat, first, count):
    lane = lax.broadcasted_iota(jnp.int32, (count * C_LAT, PIX), 1)
    in_row = lane % TW
    x = lat[first : first + count].astype(F32).reshape(count * C_LAT, PIX)
    up = jnp.where(lane < TW, x, pltpu.roll(x, TW, 1))
    down = jnp.where(lane >= PIX - TW, x, pltpu.roll(x, PIX - TW, 1))
    for a, v in enumerate((up, x, down)):
        left = jnp.where(in_row == 0, v, pltpu.roll(v, 1, 1))
        right = jnp.where(in_row == TW - 1, v, pltpu.roll(v, PIX - 1, 1))
        for e, s in enumerate((left, v, right)):
            s = s.astype(BF16)
            for k in range(count):
                at = (first + k) * TAPS + (3 * a + e) * C_LAT
                cols[at : at + C_LAT, :] = s[k * C_LAT : (k + 1) * C_LAT]


def shift_rows(z, in_row, step):
    if step < 0:
        return jnp.where(in_row == 0, z, pltpu.roll(z, 1, 0))
    return jnp.where(in_row == TW - 1, z, pltpu.roll(z, PIX - 1, 0))


def decode_kernel(
    tiles,
    groups,
    lat_in,
    writer_in,
    margin_in,
    in_w_in,
    in_b_in,
    mid_w_in,
    mid_b_in,
    skip_w_in,
    head_w_in,
    head_b_in,
    written,
    blended,
    lat,
    cols,
    w_in,
    b_in,
    w_mid,
    b_mid,
    w_skip,
    w_head,
    u,
    v,
    first_out,
    acc,
    gated,
    gather,
    s_writer,
    s_margin,
    s_head_b,
    halo_send,
    halo_recv,
    all_send,
    all_recv,
    load_sem,
    chunk_sem,
    hop,
    after,
):
    tm = lax.axis_index("tm")
    tile = lax.axis_index("tile")

    core = lax.rem(tile, CORES)
    y = lax.rem(tile // CORES, SIDE)
    x = tile // (CORES * SIDE)

    def at(x, y, core):
        return (lax.rem(x, SIDE) * SIDE + lax.rem(y, SIDE)) * CORES + lax.rem(core, CORES)

    beside_core = (at(x, y, core + 1),)
    beside_x = (at(x + 1, y, core), at(x + SIDE - 1, y, core))
    beside_y = (at(x, y + 1, core), at(x, y + SIDE - 1, core))

    def tell(semaphore, peers):
        for peer in peers:
            pl.semaphore_signal(semaphore, inc=1, device_id=(tm, peer), device_id_type=MESH)

    barrier = pltpu.get_barrier_semaphore()
    relayed = min(RELAYED, groups - 2)

    @pl.when(tm >= 1)
    def _():
        pl.semaphore_signal(barrier, inc=1, device_id=(tm - 1, tile), device_id_type=MESH)

    @pl.when(tm >= relayed + 2)
    def _():
        pl.semaphore_signal(barrier, inc=1, device_id=(tm - 2, tile), device_id_type=MESH)

    @pl.when(tm < relayed)
    def _():
        pl.semaphore_signal(barrier, inc=1, device_id=(tm + 1, tile), device_id_type=MESH)

    tell(barrier, beside_core + beside_x + beside_y)

    own = pltpu.make_async_copy(lat_in.at[0], lat.at[4:6], load_sem.at[0])
    own.start()
    chunks = []

    def load_chunk(k):
        rows = slice(k * C_MID, (k + 1) * C_MID)
        chunk = []
        for lag in range(3):
            copy = pltpu.make_async_copy(
                mid_w_in.at[lag, rows], w_mid.at[lag, rows], chunk_sem.at[3 * k + lag]
            )
            copy.start()
            chunk.append(copy)
        chunks.append(chunk)

    load_chunk(0)
    loads = []
    for k, (src, dst) in enumerate(
        (
            (in_w_in, w_in),
            (in_b_in, b_in),
            (head_w_in, w_head),
            (mid_b_in, b_mid),
            (writer_in, s_writer),
            (margin_in, s_margin),
            (head_b_in, s_head_b),
            (skip_w_in, w_skip),
        )
    ):
        copy = pltpu.make_async_copy(src, dst, load_sem.at[k + 1])
        copy.start()
        loads.append(copy)
    for k in range(1, 9):
        load_chunk(k)

    def halo(d):
        return remote(
            lat_in.at[0],
            lat.at[4 - 2 * d : 6 - 2 * d],
            halo_send.at[d - 1],
            halo_recv.at[d - 1],
            lax.rem(tm + d, groups),
            tile,
        )

    def mix_weights(k):
        for copy in chunks[k]:
            copy.wait()

        @pl.loop(0, C_MID // 64)
        def _(s):
            rows = pl.ds(pl.multiple_of(k * C_MID + s * 64, 64), 64)
            even = w_mid[0, rows, :].astype(F32) + w_mid[2, rows, :].astype(F32)
            odd = w_mid[1, rows, :].astype(F32)
            u[0, rows, :] = (even + odd).astype(BF16)
            u[1, rows, :] = (even - odd).astype(BF16)

    own.wait()
    spread_columns(cols, lat, 4, 2)
    for k in range(2):
        mix_weights(k)

    expected = (
        5
        + (tm < groups - 1).astype(jnp.int32)
        + jnp.logical_and(tm >= relayed, tm < groups - 2).astype(jnp.int32)
        + jnp.logical_and(tm >= 1, tm <= relayed).astype(jnp.int32)
    )
    pl.semaphore_wait(barrier, expected)

    @pl.when(tm < groups - 1)
    def _():
        halo(1).start()

    @pl.when(jnp.logical_and(tm >= relayed, tm < groups - 2))
    def _():
        halo(2).start()

    @pl.when(jnp.logical_and(tm >= 1, tm <= relayed))
    def _():
        pl.semaphore_signal(after, inc=1, device_id=(tm - 1, tile), device_id_type=MESH)

    tell(hop.at[0], beside_core)
    for k in range(2, 7):
        mix_weights(k)
    pl.semaphore_wait(hop.at[0], 1)
    tell(hop.at[1], beside_x)

    for k in range(7, 9):
        mix_weights(k)
    for copy in loads:
        copy.wait()

    @pl.when(tm < relayed)
    def _():
        pl.semaphore_wait(after, 1)
        halo(2).start()

    weight = w_in[...].reshape(3 * TAPS, C_MID)

    def features(j):
        out = lax.dot_general(
            cols[j * TAPS : (j + 3) * TAPS, :],
            weight,
            (((0,), (0,)), ((), ())),
            preferred_element_type=F32,
        )
        out = (out + b_in[...]).astype(BF16)
        if j >= 2:
            first_out[j - 2] = out
        return silu(out.astype(F32))

    def keep(i, m):
        m = m.astype(BF16)
        v[i, TW : TW + PIX, :] = m
        v[i, 0:TW, :] = m[0:TW]
        v[i, TW + PIX : 2 * TW + PIX, :] = m[PIX - TW : PIX]

    @pl.when(tm >= 1)
    def _():
        halo(1).wait_recv()

    pl.semaphore_wait(hop.at[1], 2)
    tell(hop.at[2], beside_x)

    @pl.when(tm == 0)
    def _():
        for g in range(4):
            lat[g] = lat[4]

    spread_columns(cols, lat, 2, 2)
    act2 = features(2)
    act3 = features(3)

    @pl.when(tm >= 2)
    def _():
        halo(2).wait_recv()

    pl.semaphore_wait(hop.at[2], 2)
    tell(hop.at[3], beside_y)

    @pl.when(tm == 1)
    def _():
        for g in range(2):
            lat[g] = lat[2]

    spread_columns(cols, lat, 0, 2)
    act1 = features(1)
    keep(1, 0.5 * (act1 + act2))
    keep(2, 0.5 * (act2 - act1))
    keep(3, act1 - act3)
    keep(0, features(0) - act2)

    in_row = lax.broadcasted_iota(jnp.int32, (PIX, C_OUT), 0) % TW

    def product(i, e):
        frames, weights = [], []
        for r in range(3):
            rows = slice((3 * r + e) * C_MID, (3 * r + e + 1) * C_MID)
            frames.append(v[i, TW * r : TW * r + PIX, :])
            if i in (0, 3):
                weights.append(w_mid[0 if i == 0 else 2, rows, :])
            else:
                weights.append(u[i - 1, rows, :])
        return jnp.dot(
            jnp.concatenate(frames, axis=1),
            jnp.concatenate(weights, axis=0),
            preferred_element_type=F32,
        )

    def finish(f, sums):
        total = sums[1] + shift_rows(sums[0], in_row, -1) + shift_rows(sums[2], in_row, 1)
        total = total + jnp.dot(first_out[f], w_skip[...], preferred_element_type=F32) + b_mid[...]
        gated[:, f * C_OUT : (f + 1) * C_OUT] = silu(total).astype(BF16)

    for e in range(3):
        p1 = product(1, e)
        acc[0, e] = p1
        acc[1, e] = p1
    for e in range(3):
        p2 = product(2, e)
        acc[0, e] += p2
        acc[1, e] -= p2
    finish(0, [acc[0, e] + product(0, e) for e in range(3)])
    finish(1, [acc[1, e] - product(3, e) for e in range(3)])

    row = lax.broadcasted_iota(jnp.int32, (8, C_OUT), 0)
    head = w_head[...].astype(F32)
    by_color = jnp.where(
        row // 2 == 0,
        head[0:1],
        jnp.where(row // 2 == 1, head[1:2], jnp.where(row // 2 == 2, head[2:3], 0.0)),
    )
    head2 = jnp.concatenate(
        [jnp.where(row % 2 == 0, by_color, 0.0), jnp.where(row % 2 == 1, by_color, 0.0)], axis=1
    ).astype(BF16)
    pixels = lax.dot_general(
        head2, gated[...], (((1,), (1,)), ((), ())), preferred_element_type=F32
    )
    pixels = pixels + jnp.where(
        row // 2 == 0, s_head_b[0], jnp.where(row // 2 == 1, s_head_b[1], s_head_b[2])
    )
    gather[tile] = jnp.concatenate([pixels[:, :128], pixels[:, 128:]], axis=0).astype(BF16)

    pl.semaphore_wait(hop.at[3], 2)
    for dx, dy, dc in FAR_FIRST:
        to = at(x + dx, y + dy, core + dc)
        remote(gather.at[tile], gather.at[tile], all_send, all_recv, tm, to).start()
    everyone = remote(
        gather.at[0 : tiles - 1],
        gather.at[0 : tiles - 1],
        all_send,
        all_recv,
        tm,
        lax.rem(tile + 1, tiles),
    )

    found = jnp.int32(0)
    which = [jnp.int32(0)] * MAXLOAD
    taken = [jnp.int32(0)] * MAXLOAD
    for t in range(tiles):
        mine = s_writer[t] == tile
        for j in range(MAXLOAD):
            hit = jnp.logical_and(mine, found == j)
            which[j] = jnp.where(hit, t, which[j])
            taken[j] = jnp.where(hit, 1, taken[j])
        found = found + mine.astype(jnp.int32)

    everyone.wait_recv()

    def tile_pixels(t):
        block = gather[t].astype(F32)
        return jnp.concatenate([block[0:8], block[8:16]], axis=1)

    for j in range(MAXLOAD):
        live = jnp.full((8, PIX), taken[j], jnp.int32) > 0
        block = jnp.where(live, tile_pixels(which[j]), 0.0).astype(BF16)
        for c in range(3):
            written[j, c] = block[2 * c : 2 * c + 2]
    width = jnp.full((8, PIX), s_margin[0], jnp.int32)
    column = lax.broadcasted_iota(jnp.int32, (8, PIX), 1) % TW
    current = tile_pixels(tile)
    before = tile_pixels(jnp.maximum(tile - 1, 0))
    prior = pltpu.roll(before, PIX - TW + MARGIN_LO, 1)
    for m in range(MARGIN_LO + 1, MARGIN_HI + 1):
        prior = jnp.where(width == m, pltpu.roll(before, PIX - TW + m, 1), prior)
    fraction = column.astype(F32) / jnp.maximum(width, 1).astype(F32)
    mix = jnp.where(column < width, (1.0 - fraction) * prior + fraction * current, current)
    mix = mix.astype(BF16)
    for c in range(3):
        blended[0, c] = mix[2 * c : 2 * c + 2]
    everyone.wait_send()
    for d in (1, 2):

        @pl.when(tm < groups - d)
        def _():
            halo(d).wait_send()


def copy_kernel(written_in, blended_in, written_out, blended_out, sem):
    copies = [
        pltpu.make_async_copy(written_in, written_out, sem.at[0]),
        pltpu.make_async_copy(blended_in, blended_out, sem.at[1]),
    ]
    for copy in copies:
        copy.start()
    for copy in copies:
        copy.wait()


def per_device(
    latents,
    writer,
    margin_cols,
    in_weight,
    in_bias,
    mid_weight,
    mid_bias,
    skip_weight,
    head_weight,
    head_bias,
):
    tiles = lax.axis_size("tile")
    groups = lax.axis_size("tm")
    frames = latents.shape[1]
    shapes = (
        jax.ShapeDtypeStruct((MAXLOAD, 3, frames, PIX), BF16),
        jax.ShapeDtypeStruct((1, 3, frames, PIX), BF16),
    )
    anywhere = pl.BlockSpec(memory_space=pl.ANY)

    def body(*refs):
        decode_kernel(tiles, groups, *refs)

    written, blended = pl.pallas_call(
        body,
        out_shape=tuple(pltpu.VMEM(s.shape, s.dtype) for s in shapes),
        in_specs=[anywhere] * 10,
        out_specs=(pl.BlockSpec(memory_space=pltpu.VMEM),) * 2,
        scratch_shapes=[
            pltpu.VMEM((6, C_LAT, PIX), BF16),
            pltpu.VMEM((6 * TAPS, PIX), BF16),
            pltpu.VMEM((3, TAPS, C_MID), BF16),
            pltpu.VMEM((1, C_MID), F32),
            pltpu.VMEM((3, 9 * C_MID, C_OUT), BF16),
            pltpu.VMEM((1, C_OUT), F32),
            pltpu.VMEM((C_MID, C_OUT), BF16),
            pltpu.VMEM((3, C_OUT), BF16),
            pltpu.VMEM((2, 9 * C_MID, C_OUT), BF16),
            pltpu.VMEM((4, PIX + 2 * TW, C_MID), BF16),
            pltpu.VMEM((2, PIX, C_MID), BF16),
            pltpu.VMEM((2, 3, PIX, C_OUT), F32),
            pltpu.VMEM((PIX, 2 * C_OUT), BF16),
            pltpu.VMEM((tiles, 16, 128), BF16),
            pltpu.SMEM((tiles,), jnp.int32),
            pltpu.SMEM((1,), jnp.int32),
            pltpu.SMEM((3,), F32),
            pltpu.SemaphoreType.DMA((2,)),
            pltpu.SemaphoreType.DMA((2,)),
            pltpu.SemaphoreType.DMA,
            pltpu.SemaphoreType.DMA,
            pltpu.SemaphoreType.DMA((9,)),
            pltpu.SemaphoreType.DMA((27,)),
            pltpu.SemaphoreType.REGULAR((4,)),
            pltpu.SemaphoreType.REGULAR,
        ],
        compiler_params=pltpu.CompilerParams(
            collective_id=0, has_side_effects=True, vmem_limit_bytes=60 * 2**20
        ),
        name="decode",
    )(
        *(
            a if a is margin_cols else pltpu.with_memory_space_constraint(a, pltpu.HBM)
            for a in (
                latents,
                writer,
                margin_cols,
                in_weight,
                in_bias.reshape(1, -1),
                mid_weight,
                mid_bias.reshape(1, -1),
                skip_weight,
                head_weight.T,
                head_bias,
            )
        )
    )
    written, blended = pl.pallas_call(
        copy_kernel,
        out_shape=shapes,
        in_specs=[anywhere] * 2,
        out_specs=(anywhere,) * 2,
        scratch_shapes=[pltpu.SemaphoreType.DMA((2,))],
        name="hand_out",
    )(
        pltpu.with_memory_space_constraint(written, pltpu.VMEM),
        pltpu.with_memory_space_constraint(blended, pltpu.VMEM),
    )
    return written.transpose(0, 2, 1, 3), blended.transpose(0, 2, 1, 3)


def solution(mesh):
    return jax.shard_map(
        per_device,
        mesh=mesh,
        in_specs=(P("tile", "tm", None, None), P(), P("tile"), P(), P(), P(), P(), P(), P(), P()),
        out_specs=(P("tile", "tm", None, None), P("tile", "tm", None, None)),
        check_vma=False,
    )
```

```python
import jax
import jax.numpy as jnp
from jax import lax
from jax.experimental import pallas as pl
from jax.experimental.pallas import tpu as pltpu
from jax.sharding import PartitionSpec as P

TH = 16
TW = 16
PIX = TH * TW
C_LAT = 16
C_MID = 512
C_OUT = 256
TAPS = 9 * C_LAT
MAXLOAD = 3
MARGIN_LO = 2
MARGIN_HI = 4
SIDE = 4
CORES = 2
MESH = pl.DeviceIdType.MESH
RELAYED = 2
FAR_FIRST = sorted(
    (
        (dx, dy, dc)
        for dx in range(SIDE)
        for dy in range(SIDE)
        for dc in range(CORES)
        if dx or dy or dc
    ),
    key=lambda p: -min(p[0], SIDE - p[0]) - min(p[1], SIDE - p[1]),
)
F32 = jnp.float32
BF16 = jnp.bfloat16


def silu(v):
    return 0.5 * v * (1.0 + jnp.tanh(0.5 * v))


def remote(src, dst, send_sem, recv_sem, tm, tile):
    return pltpu.make_async_remote_copy(
        src_ref=src,
        dst_ref=dst,
        send_sem=send_sem,
        recv_sem=recv_sem,
        device_id=(tm, tile),
        device_id_type=MESH,
    )


def spread_columns(cols, lat, first, count):
    lane = lax.broadcasted_iota(jnp.int32, (count * C_LAT, PIX), 1)
    in_row = lane % TW
    x = lat[first : first + count].astype(F32).reshape(count * C_LAT, PIX)
    up = jnp.where(lane < TW, x, pltpu.roll(x, TW, 1))
    down = jnp.where(lane >= PIX - TW, x, pltpu.roll(x, PIX - TW, 1))
    for a, v in enumerate((up, x, down)):
        left = jnp.where(in_row == 0, v, pltpu.roll(v, 1, 1))
        right = jnp.where(in_row == TW - 1, v, pltpu.roll(v, PIX - 1, 1))
        for e, s in enumerate((left, v, right)):
            s = s.astype(BF16)
            for k in range(count):
                at = (first + k) * TAPS + (3 * a + e) * C_LAT
                cols[at : at + C_LAT, :] = s[k * C_LAT : (k + 1) * C_LAT]


def shift_rows(z, in_row, step):
    if step < 0:
        return jnp.where(in_row == 0, z, pltpu.roll(z, 1, 0))
    return jnp.where(in_row == TW - 1, z, pltpu.roll(z, PIX - 1, 0))


def decode_kernel(
    tiles,
    groups,
    lat_in,
    writer_in,
    margin_in,
    in_w_in,
    in_b_in,
    mid_w_in,
    mid_b_in,
    skip_w_in,
    head_w_in,
    head_b_in,
    written,
    blended,
    lat,
    cols,
    w_in,
    b_in,
    w_mid,
    b_mid,
    w_skip,
    w_head,
    u,
    v,
    first_out,
    acc,
    gated,
    gather,
    s_writer,
    s_margin,
    s_head_b,
    halo_send,
    halo_recv,
    all_send,
    all_recv,
    load_sem,
    chunk_sem,
    hop,
    after,
):
    tm = lax.axis_index("tm")
    tile = lax.axis_index("tile")

    core = lax.rem(tile, CORES)
    y = lax.rem(tile // CORES, SIDE)
    x = tile // (CORES * SIDE)

    def at(x, y, core):
        return (lax.rem(x, SIDE) * SIDE + lax.rem(y, SIDE)) * CORES + lax.rem(core, CORES)

    row = tuple(
        at(x + dx, y, core + dc) for dx in range(SIDE) for dc in range(CORES) if dx or dc
    )
    column = tuple(at(x, y + dy, core) for dy in range(1, SIDE))

    def tell(semaphore, peers):
        for peer in peers:
            pl.semaphore_signal(semaphore, inc=1, device_id=(tm, peer), device_id_type=MESH)

    barrier = pltpu.get_barrier_semaphore()
    relayed = min(RELAYED, groups - 2)
    handed = relayed + 1

    @pl.when(tm >= 1)
    def _():
        pl.semaphore_signal(barrier, inc=1, device_id=(tm - 1, tile), device_id_type=MESH)

    @pl.when(tm >= handed + 2)
    def _():
        pl.semaphore_signal(barrier, inc=1, device_id=(tm - 2, tile), device_id_type=MESH)

    @pl.when(tm < relayed)
    def _():
        pl.semaphore_signal(barrier, inc=1, device_id=(tm + 1, tile), device_id_type=MESH)


    own = pltpu.make_async_copy(lat_in.at[0], lat.at[4:6], load_sem.at[0])
    own.start()

    def chunk(k):
        rows = slice(k * C_MID, (k + 1) * C_MID)
        return [
            pltpu.make_async_copy(
                mid_w_in.at[lag, rows], w_mid.at[lag, rows], chunk_sem.at[3 * k + lag]
            )
            for lag in range(3)
        ]

    def load_chunk(k):
        for copy in chunk(k):
            copy.start(priority=1)

    load_chunk(0)
    loads = []
    for k, (src, dst) in enumerate(
        (
            (in_w_in, w_in),
            (in_b_in, b_in),
            (head_w_in, w_head),
            (mid_b_in, b_mid),
            (writer_in, s_writer),
            (margin_in, s_margin),
            (head_b_in, s_head_b),
            (skip_w_in, w_skip),
        )
    ):
        copy = pltpu.make_async_copy(src, dst, load_sem.at[k + 1])
        copy.start()
        loads.append(copy)
    for k in range(1, 9):
        load_chunk(k)

    tell(barrier, row + column)


    def halo(d):
        return remote(
            lat.at[4:6],
            lat.at[4 - 2 * d : 6 - 2 * d],
            halo_send.at[d - 1],
            halo_recv.at[d - 1],
            lax.rem(tm + d, groups),
            tile,
        )

    def hand_on():
        return remote(
            lat.at[2:4],
            lat.at[0:2],
            halo_send.at[2],
            halo_recv.at[1],
            lax.rem(tm + 1, groups),
            tile,
        )

    def mix_weights(k):
        for copy in chunk(k):
            copy.wait()

        @pl.loop(0, C_MID // 64)
        def _(s):
            rows = pl.ds(pl.multiple_of(k * C_MID + s * 64, 64), 64)
            even = w_mid[0, rows, :].astype(F32) + w_mid[2, rows, :].astype(F32)
            odd = w_mid[1, rows, :].astype(F32)
            u[0, rows, :] = (even + odd).astype(BF16)
            u[1, rows, :] = (even - odd).astype(BF16)

    own.wait()
    spread_columns(cols, lat, 4, 2)
    mix_weights(0)

    @pl.when(tm == handed)
    def _():
        for k in range(1, 6):
            mix_weights(k)

    expected = (
        len(row + column)
        + (tm < groups - 1).astype(jnp.int32)
        + jnp.logical_and(tm >= handed, tm < groups - 2).astype(jnp.int32)
        + jnp.logical_and(tm >= 1, tm <= relayed).astype(jnp.int32)
    )
    pl.semaphore_wait(barrier, expected)

    @pl.when(tm < groups - 1)
    def _():
        halo(1).start()

    @pl.when(jnp.logical_and(tm >= handed, tm < groups - 2))
    def _():
        halo(2).start()

    @pl.when(jnp.logical_and(tm >= 1, tm <= relayed))
    def _():
        pl.semaphore_signal(after, inc=1, device_id=(tm - 1, tile), device_id_type=MESH)

    tell(hop, column)

    @pl.when(tm != handed)
    def _():
        for k in range(1, 6):
            mix_weights(k)

    @pl.when(tm == handed)
    def _():
        halo(1).wait_recv()
        hand_on().start()

    for k in range(6, 9):
        mix_weights(k)
    for copy in loads:
        copy.wait()

    @pl.when(tm < relayed)
    def _():
        pl.semaphore_wait(after, 1)
        halo(2).start()

    weight = w_in[...].reshape(3 * TAPS, C_MID)

    def features(j):
        out = lax.dot_general(
            cols[j * TAPS : (j + 3) * TAPS, :],
            weight,
            (((0,), (0,)), ((), ())),
            preferred_element_type=F32,
        )
        out = (out + b_in[...]).astype(BF16)
        if j >= 2:
            first_out[j - 2] = out
        return silu(out.astype(F32))

    def keep(i, m):
        m = m.astype(BF16)
        v[i, TW : TW + PIX, :] = m
        v[i, 0:TW, :] = m[0:TW]
        v[i, TW + PIX : 2 * TW + PIX, :] = m[PIX - TW : PIX]

    @pl.when(jnp.logical_and(tm >= 1, tm != handed))
    def _():
        halo(1).wait_recv()

    @pl.when(tm == 0)
    def _():
        for g in range(4):
            lat[g] = lat[4]

    spread_columns(cols, lat, 2, 2)
    act2 = features(2)
    act3 = features(3)

    @pl.when(tm >= 2)
    def _():
        halo(2).wait_recv()

    @pl.when(tm == 1)
    def _():
        for g in range(2):
            lat[g] = lat[2]

    spread_columns(cols, lat, 0, 2)
    act1 = features(1)
    keep(1, 0.5 * (act1 + act2))
    keep(2, 0.5 * (act2 - act1))
    keep(3, act1 - act3)
    keep(0, features(0) - act2)

    in_row = lax.broadcasted_iota(jnp.int32, (PIX, C_OUT), 0) % TW

    def product(i, e):
        frames, weights = [], []
        for r in range(3):
            rows = slice((3 * r + e) * C_MID, (3 * r + e + 1) * C_MID)
            frames.append(v[i, TW * r : TW * r + PIX, :])
            if i in (0, 3):
                weights.append(w_mid[0 if i == 0 else 2, rows, :])
            else:
                weights.append(u[i - 1, rows, :])
        return jnp.dot(
            jnp.concatenate(frames, axis=1),
            jnp.concatenate(weights, axis=0),
            preferred_element_type=F32,
        )

    def finish(f, sums):
        total = sums[1] + shift_rows(sums[0], in_row, -1) + shift_rows(sums[2], in_row, 1)
        total = total + jnp.dot(first_out[f], w_skip[...], preferred_element_type=F32) + b_mid[...]
        gated[:, f * C_OUT : (f + 1) * C_OUT] = silu(total).astype(BF16)

    for e in range(3):
        p1 = product(1, e)
        acc[0, e] = p1
        acc[1, e] = p1
    for e in range(3):
        p2 = product(2, e)
        acc[0, e] += p2
        acc[1, e] -= p2
    finish(0, [acc[0, e] + product(0, e) for e in range(3)])
    finish(1, [acc[1, e] - product(3, e) for e in range(3)])

    row = lax.broadcasted_iota(jnp.int32, (8, C_OUT), 0)
    head = w_head[...].astype(F32)
    by_color = jnp.where(
        row // 2 == 0,
        head[0:1],
        jnp.where(row // 2 == 1, head[1:2], jnp.where(row // 2 == 2, head[2:3], 0.0)),
    )
    head2 = jnp.concatenate(
        [jnp.where(row % 2 == 0, by_color, 0.0), jnp.where(row % 2 == 1, by_color, 0.0)], axis=1
    ).astype(BF16)
    pixels = lax.dot_general(
        head2, gated[...], (((1,), (1,)), ((), ())), preferred_element_type=F32
    )
    pixels = pixels + jnp.where(
        row // 2 == 0, s_head_b[0], jnp.where(row // 2 == 1, s_head_b[1], s_head_b[2])
    )
    gather[tile] = jnp.concatenate([pixels[:, :128], pixels[:, 128:]], axis=0).astype(BF16)

    pl.semaphore_wait(hop, len(column))
    for dx, dy, dc in FAR_FIRST:
        to = at(x + dx, y + dy, core + dc)
        remote(gather.at[tile], gather.at[tile], all_send, all_recv, tm, to).start()
    everyone = remote(
        gather.at[0 : tiles - 1],
        gather.at[0 : tiles - 1],
        all_send,
        all_recv,
        tm,
        lax.rem(tile + 1, tiles),
    )

    found = jnp.int32(0)
    which = [jnp.int32(0)] * MAXLOAD
    taken = [jnp.int32(0)] * MAXLOAD
    for t in range(tiles):
        mine = s_writer[t] == tile
        for j in range(MAXLOAD):
            hit = jnp.logical_and(mine, found == j)
            which[j] = jnp.where(hit, t, which[j])
            taken[j] = jnp.where(hit, 1, taken[j])
        found = found + mine.astype(jnp.int32)

    everyone.wait_recv()

    def tile_pixels(t):
        block = gather[t].astype(F32)
        return jnp.concatenate([block[0:8], block[8:16]], axis=1)

    for j in range(MAXLOAD):
        live = jnp.full((8, PIX), taken[j], jnp.int32) > 0
        block = jnp.where(live, tile_pixels(which[j]), 0.0).astype(BF16)
        for c in range(3):
            written[j, c] = block[2 * c : 2 * c + 2]
    width = jnp.full((8, PIX), s_margin[0], jnp.int32)
    column = lax.broadcasted_iota(jnp.int32, (8, PIX), 1) % TW
    current = tile_pixels(tile)
    before = tile_pixels(jnp.maximum(tile - 1, 0))
    prior = pltpu.roll(before, PIX - TW + MARGIN_LO, 1)
    for m in range(MARGIN_LO + 1, MARGIN_HI + 1):
        prior = jnp.where(width == m, pltpu.roll(before, PIX - TW + m, 1), prior)
    fraction = column.astype(F32) / jnp.maximum(width, 1).astype(F32)
    mix = jnp.where(column < width, (1.0 - fraction) * prior + fraction * current, current)
    mix = mix.astype(BF16)
    for c in range(3):
        blended[0, c] = mix[2 * c : 2 * c + 2]
    everyone.wait_send()

    @pl.when(tm < groups - 1)
    def _():
        halo(1).wait_send()

    @pl.when(jnp.logical_and(tm != relayed, tm < groups - 2))
    def _():
        halo(2).wait_send()

    @pl.when(tm == handed)
    def _():
        hand_on().wait_send()


def copy_kernel(written_in, blended_in, written_out, blended_out, sem):
    copies = [
        pltpu.make_async_copy(written_in, written_out, sem.at[0]),
        pltpu.make_async_copy(blended_in, blended_out, sem.at[1]),
    ]
    for copy in copies:
        copy.start()
    for copy in copies:
        copy.wait()


def per_device(
    latents,
    writer,
    margin_cols,
    in_weight,
    in_bias,
    mid_weight,
    mid_bias,
    skip_weight,
    head_weight,
    head_bias,
):
    tiles = lax.axis_size("tile")
    groups = lax.axis_size("tm")
    frames = latents.shape[1]
    shapes = (
        jax.ShapeDtypeStruct((MAXLOAD, 3, frames, PIX), BF16),
        jax.ShapeDtypeStruct((1, 3, frames, PIX), BF16),
    )
    anywhere = pl.BlockSpec(memory_space=pl.ANY)

    def body(*refs):
        decode_kernel(tiles, groups, *refs)

    written, blended = pl.pallas_call(
        body,
        out_shape=tuple(pltpu.VMEM(s.shape, s.dtype) for s in shapes),
        in_specs=[anywhere] * 10,
        out_specs=(pl.BlockSpec(memory_space=pltpu.VMEM),) * 2,
        scratch_shapes=[
            pltpu.VMEM((6, C_LAT, PIX), BF16),
            pltpu.VMEM((6 * TAPS, PIX), BF16),
            pltpu.VMEM((3, TAPS, C_MID), BF16),
            pltpu.VMEM((1, C_MID), F32),
            pltpu.VMEM((3, 9 * C_MID, C_OUT), BF16),
            pltpu.VMEM((1, C_OUT), F32),
            pltpu.VMEM((C_MID, C_OUT), BF16),
            pltpu.VMEM((3, C_OUT), BF16),
            pltpu.VMEM((2, 9 * C_MID, C_OUT), BF16),
            pltpu.VMEM((4, PIX + 2 * TW, C_MID), BF16),
            pltpu.VMEM((2, PIX, C_MID), BF16),
            pltpu.VMEM((2, 3, PIX, C_OUT), F32),
            pltpu.VMEM((PIX, 2 * C_OUT), BF16),
            pltpu.VMEM((tiles, 16, 128), BF16),
            pltpu.SMEM((tiles,), jnp.int32),
            pltpu.SMEM((1,), jnp.int32),
            pltpu.SMEM((3,), F32),
            pltpu.SemaphoreType.DMA((3,)),
            pltpu.SemaphoreType.DMA((2,)),
            pltpu.SemaphoreType.DMA,
            pltpu.SemaphoreType.DMA,
            pltpu.SemaphoreType.DMA((9,)),
            pltpu.SemaphoreType.DMA((27,)),
            pltpu.SemaphoreType.REGULAR,
            pltpu.SemaphoreType.REGULAR,
        ],
        compiler_params=pltpu.CompilerParams(
            collective_id=0, has_side_effects=True, vmem_limit_bytes=60 * 2**20
        ),
        name="decode",
    )(
        *(
            a if a is margin_cols else pltpu.with_memory_space_constraint(a, pltpu.HBM)
            for a in (
                latents,
                writer,
                margin_cols,
                in_weight,
                in_bias.reshape(1, -1),
                mid_weight,
                mid_bias.reshape(1, -1),
                skip_weight,
                head_weight.T,
                head_bias,
            )
        )
    )
    written, blended = pl.pallas_call(
        copy_kernel,
        out_shape=shapes,
        in_specs=[anywhere] * 2,
        out_specs=(anywhere,) * 2,
        scratch_shapes=[pltpu.SemaphoreType.DMA((2,))],
        name="hand_out",
    )(
        pltpu.with_memory_space_constraint(written, pltpu.VMEM),
        pltpu.with_memory_space_constraint(blended, pltpu.VMEM),
    )
    return written.transpose(0, 2, 1, 3), blended.transpose(0, 2, 1, 3)


def solution(mesh):
    return jax.shard_map(
        per_device,
        mesh=mesh,
        in_specs=(P("tile", "tm", None, None), P(), P("tile"), P(), P(), P(), P(), P(), P(), P()),
        out_specs=(P("tile", "tm", None, None), P("tile", "tm", None, None)),
        check_vma=False,
    )
```

```python
import jax
import jax.numpy as jnp
from jax import lax
from jax.experimental import pallas as pl
from jax.experimental.pallas import tpu as pltpu
from jax.sharding import PartitionSpec as P

TH = 16
TW = 16
PIX = TH * TW
C_LAT = 16
C_MID = 512
C_OUT = 256
TAPS = 9 * C_LAT
MAXLOAD = 3
MARGIN_LO = 2
MARGIN_HI = 4
SIDE = 4
CORES = 2
MESH = pl.DeviceIdType.MESH
RELAYED = 2
PAIRS = TH // 2
HALF = PIX // 2
STEP = 16
PARTS = ((0, 0, C_MID), (1, 0, C_MID), (2, 0, C_MID // 2), (2, C_MID // 2, C_MID // 2))
MIXED = tuple((i, r) for i in range(4) for r in range(4) if i in (1, 2) or r in (1, 2))
FAR_FIRST = sorted(
    (
        (dx, dy, dc)
        for dx in range(SIDE)
        for dy in range(SIDE)
        for dc in range(CORES)
        if dx or dy or dc
    ),
    key=lambda p: -min(p[0], SIDE - p[0]) - min(p[1], SIDE - p[1]),
)
F32 = jnp.float32
BF16 = jnp.bfloat16


def silu(v):
    return 0.5 * v * (1.0 + jnp.tanh(0.5 * v))


def remote(src, dst, send_sem, recv_sem, tm, tile):
    return pltpu.make_async_remote_copy(
        src_ref=src,
        dst_ref=dst,
        send_sem=send_sem,
        recv_sem=recv_sem,
        device_id=(tm, tile),
        device_id_type=MESH,
    )


def spread_columns(cols, lat, first, count):
    lane = lax.broadcasted_iota(jnp.int32, (count * C_LAT, PIX), 1)
    in_row = lane % TW
    x = lat[first : first + count].astype(F32).reshape(count * C_LAT, PIX)
    up = jnp.where(lane < TW, x, pltpu.roll(x, TW, 1))
    down = jnp.where(lane >= PIX - TW, x, pltpu.roll(x, PIX - TW, 1))
    for a, v in enumerate((up, x, down)):
        left = jnp.where(in_row == 0, v, pltpu.roll(v, 1, 1))
        right = jnp.where(in_row == TW - 1, v, pltpu.roll(v, PIX - 1, 1))
        for e, s in enumerate((left, v, right)):
            s = s.astype(BF16)
            for k in range(count):
                at = (first + k) * TAPS + (3 * a + e) * C_LAT
                cols[at : at + C_LAT, :] = s[k * C_LAT : (k + 1) * C_LAT]


def shift_rows(z, in_row, step):
    if step < 0:
        return jnp.where(in_row == 0, z, pltpu.roll(z, 1, 0))
    return jnp.where(in_row == TW - 1, z, pltpu.roll(z, HALF - 1, 0))


def decode_kernel(
    tiles,
    groups,
    lat_in,
    writer_in,
    margin_in,
    in_w_in,
    in_b_in,
    mid_w_in,
    mid_b_in,
    skip_w_in,
    head_w_in,
    head_b_in,
    written,
    blended,
    lat,
    cols,
    w_in,
    b_in,
    w_mid,
    b_mid,
    w_skip,
    w_head,
    u,
    v,
    first_out,
    acc,
    base,
    terms,
    gated,
    gather,
    s_writer,
    s_margin,
    s_head_b,
    halo_send,
    halo_recv,
    all_send,
    all_recv,
    load_sem,
    chunk_sem,
    hop,
    after,
):
    tm = lax.axis_index("tm")
    tile = lax.axis_index("tile")

    core = lax.rem(tile, CORES)
    y = lax.rem(tile // CORES, SIDE)
    x = tile // (CORES * SIDE)

    def at(x, y, core):
        return (lax.rem(x, SIDE) * SIDE + lax.rem(y, SIDE)) * CORES + lax.rem(core, CORES)

    row = tuple(
        at(x + dx, y, core + dc) for dx in range(SIDE) for dc in range(CORES) if dx or dc
    )
    column = tuple(at(x, y + dy, core) for dy in range(1, SIDE))

    def tell(semaphore, peers):
        for peer in peers:
            pl.semaphore_signal(semaphore, inc=1, device_id=(tm, peer), device_id_type=MESH)

    barrier = pltpu.get_barrier_semaphore()
    relayed = min(RELAYED, groups - 2)
    handed = relayed + 1

    @pl.when(tm >= 1)
    def _():
        pl.semaphore_signal(barrier, inc=1, device_id=(tm - 1, tile), device_id_type=MESH)

    @pl.when(tm >= handed + 2)
    def _():
        pl.semaphore_signal(barrier, inc=1, device_id=(tm - 2, tile), device_id_type=MESH)

    @pl.when(tm < relayed)
    def _():
        pl.semaphore_signal(barrier, inc=1, device_id=(tm + 1, tile), device_id_type=MESH)


    own = pltpu.make_async_copy(lat_in.at[0], lat.at[4:6], load_sem.at[0])
    own.start()

    def part(k):
        column, first, count = PARTS[k]
        copies = []
        for a in range(3):
            for lag in range(3):
                rows = pl.ds((3 * a + column) * C_MID + first, count)
                copies.append(
                    pltpu.make_async_copy(
                        mid_w_in.at[lag, rows],
                        w_mid.at[lag, rows],
                        chunk_sem.at[9 * k + 3 * a + lag],
                    )
                )
        return copies

    def load_part(k):
        for copy in part(k):
            copy.start(priority=1)

    load_part(0)
    loads = []
    for k, (src, dst) in enumerate(
        (
            (in_w_in, w_in),
            (in_b_in, b_in),
            (head_w_in, w_head),
            (mid_b_in, b_mid),
            (writer_in, s_writer),
            (margin_in, s_margin),
            (head_b_in, s_head_b),
            (skip_w_in, w_skip),
        )
    ):
        copy = pltpu.make_async_copy(src, dst, load_sem.at[k + 1])
        copy.start()
        loads.append(copy)
    for k in range(1, 4):
        load_part(k)

    tell(barrier, row + column)


    def halo(d):
        return remote(
            lat.at[4:6],
            lat.at[4 - 2 * d : 6 - 2 * d],
            halo_send.at[d - 1],
            halo_recv.at[d - 1],
            lax.rem(tm + d, groups),
            tile,
        )

    def hand_on():
        return remote(
            lat.at[2:4],
            lat.at[0:2],
            halo_send.at[2],
            halo_recv.at[1],
            lax.rem(tm + 1, groups),
            tile,
        )

    def mix(first, second, third):
        even = first + third
        return first, even + second, even - second, third

    def mix_weights(k):
        for copy in part(k):
            copy.wait()
        column, first, count = PARTS[k]

        @pl.loop(0, count // STEP)
        def _(s):
            at_row = first + s * STEP
            by_row = []
            for a in range(3):
                rows = pl.ds(pl.multiple_of((3 * a + column) * C_MID + at_row, STEP), STEP)
                by_row.append(mix(*(w_mid[lag, rows, :].astype(F32) for lag in range(3))))
            rows = pl.ds(pl.multiple_of(column * C_MID + at_row, STEP), STEP)
            for i in range(4):
                by_time = mix(*(by_row[a][i] for a in range(3)))
                for r in range(4):
                    if (i, r) in MIXED:
                        u[MIXED.index((i, r)), rows, :] = by_time[r].astype(BF16)

    own.wait()
    spread_columns(cols, lat, 4, 2)
    @pl.when(tm == handed)
    def _():
        for k in range(2):
            mix_weights(k)

    expected = (
        len(row + column)
        + (tm < groups - 1).astype(jnp.int32)
        + jnp.logical_and(tm >= handed, tm < groups - 2).astype(jnp.int32)
        + jnp.logical_and(tm >= 1, tm <= relayed).astype(jnp.int32)
    )
    pl.semaphore_wait(barrier, expected)

    @pl.when(tm < groups - 1)
    def _():
        halo(1).start()

    @pl.when(jnp.logical_and(tm >= handed, tm < groups - 2))
    def _():
        halo(2).start()

    @pl.when(jnp.logical_and(tm >= 1, tm <= relayed))
    def _():
        pl.semaphore_signal(after, inc=1, device_id=(tm - 1, tile), device_id_type=MESH)

    tell(hop, column)

    @pl.when(tm != handed)
    def _():
        for k in range(2):
            mix_weights(k)

    @pl.when(tm == handed)
    def _():
        halo(1).wait_recv()
        hand_on().start()

    for k in range(2, 4):
        mix_weights(k)
    for copy in loads:
        copy.wait()

    @pl.when(tm < relayed)
    def _():
        pl.semaphore_wait(after, 1)
        halo(2).start()

    weight = w_in[...].reshape(3 * TAPS, C_MID)

    def features(j):
        out = lax.dot_general(
            cols[j * TAPS : (j + 3) * TAPS, :],
            weight,
            (((0,), (0,)), ((), ())),
            preferred_element_type=F32,
        )
        out = (out + b_in[...]).astype(BF16)
        if j >= 2:
            by_pair = out.reshape(PAIRS, 2, TW, C_MID)
            for p in range(2):
                first_out[j - 2, p] = by_pair[:, p].reshape(HALF, C_MID)
        return silu(out.astype(F32))

    def keep(i, m):
        by_pair = m.reshape(PAIRS, 2, TW, C_MID)
        upper, lower = by_pair[:, 0], by_pair[:, 1]
        above = jnp.concatenate([upper[:1], lower[:-1]], axis=0)
        below = jnp.concatenate([upper[1:], lower[-1:]], axis=0)
        rows = (above - lower, 0.5 * (upper + lower), 0.5 * (lower - upper), upper - below)
        for r in range(4):
            v[4 * i + r] = rows[r].reshape(HALF, C_MID).astype(BF16)

    @pl.when(jnp.logical_and(tm >= 1, tm != handed))
    def _():
        halo(1).wait_recv()

    @pl.when(tm == 0)
    def _():
        for g in range(4):
            lat[g] = lat[4]

    spread_columns(cols, lat, 2, 2)
    act2 = features(2)
    act3 = features(3)
    for f in range(2):
        for p in range(2):
            base[f, p] = jnp.dot(first_out[f, p], w_skip[...], preferred_element_type=F32) + b_mid[...]

    @pl.when(tm >= 2)
    def _():
        halo(2).wait_recv()

    @pl.when(tm == 1)
    def _():
        for g in range(2):
            lat[g] = lat[2]

    spread_columns(cols, lat, 0, 2)
    act1 = features(1)
    keep(1, 0.5 * (act1 + act2))
    keep(2, 0.5 * (act2 - act1))
    keep(3, act1 - act3)
    keep(0, features(0) - act2)

    in_row = lax.broadcasted_iota(jnp.int32, (HALF, C_OUT), 0) % TW

    def product(i, r, e):
        if (i, r) in MIXED:
            weights = u[MIXED.index((i, r)), e * C_MID : (e + 1) * C_MID, :]
        else:
            tap = 6 + e if r else e
            weights = w_mid[2 if i else 0, tap * C_MID : (tap + 1) * C_MID, :]
        return jnp.dot(v[4 * i + r], weights, preferred_element_type=F32)

    def row_pair(i, e):
        for r in range(4):
            terms[i % 2, e, r] = product(i, r, e)
        p = [terms[i % 2, e, r] for r in range(4)]
        return p[0] + p[1] + p[2], p[1] - p[2] - p[3]

    def finish(f, p, sums):
        total = sums[1] + shift_rows(sums[0], in_row, -1) + shift_rows(sums[2], in_row, 1)
        total = silu(total + base[f, p]).astype(BF16)
        gated[:, p, :, f * C_OUT : (f + 1) * C_OUT] = total.reshape(PAIRS, TW, C_OUT)

    for e in range(3):
        first = row_pair(1, e)
        second = row_pair(2, e)
        for p in range(2):
            acc[0, p, e] = first[p] + second[p]
            acc[1, p, e] = first[p] - second[p]
    for f, i in ((0, 0), (1, 3)):
        last = [row_pair(i, e) for e in range(3)]
        for p in range(2):
            if f == 0:
                finish(f, p, [acc[f, p, e] + last[e][p] for e in range(3)])
            else:
                finish(f, p, [acc[f, p, e] - last[e][p] for e in range(3)])

    row = lax.broadcasted_iota(jnp.int32, (8, C_OUT), 0)
    head = w_head[...].astype(F32)
    by_color = jnp.where(
        row // 2 == 0,
        head[0:1],
        jnp.where(row // 2 == 1, head[1:2], jnp.where(row // 2 == 2, head[2:3], 0.0)),
    )
    head2 = jnp.concatenate(
        [jnp.where(row % 2 == 0, by_color, 0.0), jnp.where(row % 2 == 1, by_color, 0.0)], axis=1
    ).astype(BF16)
    pixels = lax.dot_general(
        head2, gated[...].reshape(PIX, 2 * C_OUT), (((1,), (1,)), ((), ())), preferred_element_type=F32
    )
    pixels = pixels + jnp.where(
        row // 2 == 0, s_head_b[0], jnp.where(row // 2 == 1, s_head_b[1], s_head_b[2])
    )
    gather[tile] = jnp.concatenate([pixels[:, :128], pixels[:, 128:]], axis=0).astype(BF16)

    pl.semaphore_wait(hop, len(column))
    for dx, dy, dc in FAR_FIRST:
        to = at(x + dx, y + dy, core + dc)
        remote(gather.at[tile], gather.at[tile], all_send, all_recv, tm, to).start()
    everyone = remote(
        gather.at[0 : tiles - 1],
        gather.at[0 : tiles - 1],
        all_send,
        all_recv,
        tm,
        lax.rem(tile + 1, tiles),
    )

    found = jnp.int32(0)
    which = [jnp.int32(0)] * MAXLOAD
    taken = [jnp.int32(0)] * MAXLOAD
    for t in range(tiles):
        mine = s_writer[t] == tile
        for j in range(MAXLOAD):
            hit = jnp.logical_and(mine, found == j)
            which[j] = jnp.where(hit, t, which[j])
            taken[j] = jnp.where(hit, 1, taken[j])
        found = found + mine.astype(jnp.int32)

    everyone.wait_recv()

    def tile_pixels(t):
        block = gather[t].astype(F32)
        return jnp.concatenate([block[0:8], block[8:16]], axis=1)

    for j in range(MAXLOAD):
        live = jnp.full((8, PIX), taken[j], jnp.int32) > 0
        block = jnp.where(live, tile_pixels(which[j]), 0.0).astype(BF16)
        for c in range(3):
            written[j, c] = block[2 * c : 2 * c + 2]
    width = jnp.full((8, PIX), s_margin[0], jnp.int32)
    column = lax.broadcasted_iota(jnp.int32, (8, PIX), 1) % TW
    current = tile_pixels(tile)
    before = tile_pixels(jnp.maximum(tile - 1, 0))
    prior = pltpu.roll(before, PIX - TW + MARGIN_LO, 1)
    for m in range(MARGIN_LO + 1, MARGIN_HI + 1):
        prior = jnp.where(width == m, pltpu.roll(before, PIX - TW + m, 1), prior)
    fraction = column.astype(F32) / jnp.maximum(width, 1).astype(F32)
    mix = jnp.where(column < width, (1.0 - fraction) * prior + fraction * current, current)
    mix = mix.astype(BF16)
    for c in range(3):
        blended[0, c] = mix[2 * c : 2 * c + 2]
    everyone.wait_send()

    @pl.when(tm < groups - 1)
    def _():
        halo(1).wait_send()

    @pl.when(jnp.logical_and(tm != relayed, tm < groups - 2))
    def _():
        halo(2).wait_send()

    @pl.when(tm == handed)
    def _():
        hand_on().wait_send()


def copy_kernel(written_in, blended_in, written_out, blended_out, sem):
    copies = [
        pltpu.make_async_copy(written_in, written_out, sem.at[0]),
        pltpu.make_async_copy(blended_in, blended_out, sem.at[1]),
    ]
    for copy in copies:
        copy.start()
    for copy in copies:
        copy.wait()


def per_device(
    latents,
    writer,
    margin_cols,
    in_weight,
    in_bias,
    mid_weight,
    mid_bias,
    skip_weight,
    head_weight,
    head_bias,
):
    tiles = lax.axis_size("tile")
    groups = lax.axis_size("tm")
    frames = latents.shape[1]
    shapes = (
        jax.ShapeDtypeStruct((MAXLOAD, 3, frames, PIX), BF16),
        jax.ShapeDtypeStruct((1, 3, frames, PIX), BF16),
    )
    anywhere = pl.BlockSpec(memory_space=pl.ANY)

    def body(*refs):
        decode_kernel(tiles, groups, *refs)

    written, blended = pl.pallas_call(
        body,
        out_shape=tuple(pltpu.VMEM(s.shape, s.dtype) for s in shapes),
        in_specs=[anywhere] * 10,
        out_specs=(pl.BlockSpec(memory_space=pltpu.VMEM),) * 2,
        scratch_shapes=[
            pltpu.VMEM((6, C_LAT, PIX), BF16),
            pltpu.VMEM((6 * TAPS, PIX), BF16),
            pltpu.VMEM((3, TAPS, C_MID), BF16),
            pltpu.VMEM((1, C_MID), F32),
            pltpu.VMEM((3, 9 * C_MID, C_OUT), BF16),
            pltpu.VMEM((1, C_OUT), F32),
            pltpu.VMEM((C_MID, C_OUT), BF16),
            pltpu.VMEM((3, C_OUT), BF16),
            pltpu.VMEM((len(MIXED), 3 * C_MID, C_OUT), BF16),
            pltpu.VMEM((16, HALF, C_MID), BF16),
            pltpu.VMEM((2, 2, HALF, C_MID), BF16),
            pltpu.VMEM((2, 2, 3, HALF, C_OUT), F32),
            pltpu.VMEM((2, 2, HALF, C_OUT), F32),
            pltpu.VMEM((2, 3, 4, HALF, C_OUT), F32),
            pltpu.VMEM((PAIRS, 2, TW, 2 * C_OUT), BF16),
            pltpu.VMEM((tiles, 16, 128), BF16),
            pltpu.SMEM((tiles,), jnp.int32),
            pltpu.SMEM((1,), jnp.int32),
            pltpu.SMEM((3,), F32),
            pltpu.SemaphoreType.DMA((3,)),
            pltpu.SemaphoreType.DMA((2,)),
            pltpu.SemaphoreType.DMA,
            pltpu.SemaphoreType.DMA,
            pltpu.SemaphoreType.DMA((9,)),
            pltpu.SemaphoreType.DMA((36,)),
            pltpu.SemaphoreType.REGULAR,
            pltpu.SemaphoreType.REGULAR,
        ],
        compiler_params=pltpu.CompilerParams(
            collective_id=0, has_side_effects=True, vmem_limit_bytes=60 * 2**20
        ),
        name="decode",
    )(
        *(
            a if a is margin_cols else pltpu.with_memory_space_constraint(a, pltpu.HBM)
            for a in (
                latents,
                writer,
                margin_cols,
                in_weight,
                in_bias.reshape(1, -1),
                mid_weight,
                mid_bias.reshape(1, -1),
                skip_weight,
                head_weight.T,
                head_bias,
            )
        )
    )
    written, blended = pl.pallas_call(
        copy_kernel,
        out_shape=shapes,
        in_specs=[anywhere] * 2,
        out_specs=(anywhere,) * 2,
        scratch_shapes=[pltpu.SemaphoreType.DMA((2,))],
        name="hand_out",
    )(
        pltpu.with_memory_space_constraint(written, pltpu.VMEM),
        pltpu.with_memory_space_constraint(blended, pltpu.VMEM),
    )
    return written.transpose(0, 2, 1, 3), blended.transpose(0, 2, 1, 3)


def solution(mesh):
    return jax.shard_map(
        per_device,
        mesh=mesh,
        in_specs=(P("tile", "tm", None, None), P(), P("tile"), P(), P(), P(), P(), P(), P(), P()),
        out_specs=(P("tile", "tm", None, None), P("tile", "tm", None, None)),
        check_vma=False,
    )
```

```python
import jax
import jax.numpy as jnp
from jax import lax
from jax.experimental import pallas as pl
from jax.experimental.pallas import tpu as pltpu
from jax.sharding import PartitionSpec as P

TH = 16
TW = 16
PIX = TH * TW
C_LAT = 16
C_MID = 512
C_OUT = 256
TAPS = 9 * C_LAT
MAXLOAD = 3
MARGIN_LO = 2
MARGIN_HI = 4
SIDE = 4
CORES = 2
MESH = pl.DeviceIdType.MESH
RELAYED = 2
PAIRS = TH // 2
HALF = PIX // 2
STEP = 32
PARTS = ((0, 0, C_MID), (1, 0, C_MID), (2, 0, C_MID // 2), (2, C_MID // 2, C_MID // 2))
MIXED = tuple((i, r) for i in range(4) for r in range(4) if i in (1, 2) or r in (1, 2))
FAR_FIRST = sorted(
    (
        (dx, dy, dc)
        for dx in range(SIDE)
        for dy in range(SIDE)
        for dc in range(CORES)
        if dx or dy or dc
    ),
    key=lambda p: -min(p[0], SIDE - p[0]) - min(p[1], SIDE - p[1]),
)
F32 = jnp.float32
BF16 = jnp.bfloat16


def silu(v):
    return 0.5 * v * (1.0 + jnp.tanh(0.5 * v))


def remote(src, dst, send_sem, recv_sem, tm, tile):
    return pltpu.make_async_remote_copy(
        src_ref=src,
        dst_ref=dst,
        send_sem=send_sem,
        recv_sem=recv_sem,
        device_id=(tm, tile),
        device_id_type=MESH,
    )


def spread_columns(cols, lat, first, count):
    lane = lax.broadcasted_iota(jnp.int32, (count * C_LAT, PIX), 1)
    in_row = lane % TW
    x = lat[first : first + count].astype(F32).reshape(count * C_LAT, PIX)
    up = jnp.where(lane < TW, x, pltpu.roll(x, TW, 1))
    down = jnp.where(lane >= PIX - TW, x, pltpu.roll(x, PIX - TW, 1))
    for a, v in enumerate((up, x, down)):
        left = jnp.where(in_row == 0, v, pltpu.roll(v, 1, 1))
        right = jnp.where(in_row == TW - 1, v, pltpu.roll(v, PIX - 1, 1))
        for e, s in enumerate((left, v, right)):
            s = s.astype(BF16)
            for k in range(count):
                at = (first + k) * TAPS + (3 * a + e) * C_LAT
                cols[at : at + C_LAT, :] = s[k * C_LAT : (k + 1) * C_LAT]


def shift_rows(z, in_row, step):
    if step < 0:
        return jnp.where(in_row == 0, z, pltpu.roll(z, 1, 0))
    return jnp.where(in_row == TW - 1, z, pltpu.roll(z, HALF - 1, 0))


def decode_kernel(
    tiles,
    groups,
    lat_in,
    writer_in,
    margin_in,
    in_w_in,
    in_b_in,
    mid_w_in,
    mid_b_in,
    skip_w_in,
    head_w_in,
    head_b_in,
    written,
    blended,
    lat,
    cols,
    w_in,
    b_in,
    w_mid,
    b_mid,
    w_skip,
    w_head,
    u,
    v,
    first_out,
    acc,
    base,
    terms,
    gated,
    gather,
    s_writer,
    s_margin,
    s_head_b,
    halo_send,
    halo_recv,
    all_send,
    all_recv,
    load_sem,
    chunk_sem,
    hop,
    after,
):
    tm = lax.axis_index("tm")
    tile = lax.axis_index("tile")

    core = lax.rem(tile, CORES)
    y = lax.rem(tile // CORES, SIDE)
    x = tile // (CORES * SIDE)

    def at(x, y, core):
        return (lax.rem(x, SIDE) * SIDE + lax.rem(y, SIDE)) * CORES + lax.rem(core, CORES)

    row = tuple(
        at(x + dx, y, core + dc) for dx in range(SIDE) for dc in range(CORES) if dx or dc
    )
    column = tuple(at(x, y + dy, core) for dy in range(1, SIDE))

    def tell(semaphore, peers):
        for peer in peers:
            pl.semaphore_signal(semaphore, inc=1, device_id=(tm, peer), device_id_type=MESH)

    barrier = pltpu.get_barrier_semaphore()
    relayed = min(RELAYED, groups - 2)
    handed = relayed + 1

    @pl.when(tm >= 1)
    def _():
        pl.semaphore_signal(barrier, inc=1, device_id=(tm - 1, tile), device_id_type=MESH)

    @pl.when(tm >= handed + 2)
    def _():
        pl.semaphore_signal(barrier, inc=1, device_id=(tm - 2, tile), device_id_type=MESH)

    @pl.when(tm < relayed)
    def _():
        pl.semaphore_signal(barrier, inc=1, device_id=(tm + 1, tile), device_id_type=MESH)


    own = pltpu.make_async_copy(lat_in.at[0], lat.at[4:6], load_sem.at[0])
    own.start()

    def part(k):
        column, first, count = PARTS[k]
        copies = []
        for a in range(3):
            for lag in range(3):
                rows = pl.ds((3 * a + column) * C_MID + first, count)
                copies.append(
                    pltpu.make_async_copy(
                        mid_w_in.at[lag, rows],
                        w_mid.at[lag, rows],
                        chunk_sem.at[9 * k + 3 * a + lag],
                    )
                )
        return copies

    def load_part(k):
        for copy in part(k):
            copy.start(priority=1)

    load_part(0)
    loads = []
    for k, (src, dst) in enumerate(
        (
            (in_w_in, w_in),
            (in_b_in, b_in),
            (head_w_in, w_head),
            (mid_b_in, b_mid),
            (writer_in, s_writer),
            (margin_in, s_margin),
            (head_b_in, s_head_b),
            (skip_w_in, w_skip),
        )
    ):
        copy = pltpu.make_async_copy(src, dst, load_sem.at[k + 1])
        copy.start()
        loads.append(copy)
    for k in range(1, 4):
        load_part(k)

    tell(barrier, row + column)


    def halo(d):
        return remote(
            lat.at[4:6],
            lat.at[4 - 2 * d : 6 - 2 * d],
            halo_send.at[d - 1],
            halo_recv.at[d - 1],
            lax.rem(tm + d, groups),
            tile,
        )

    def hand_on():
        return remote(
            lat.at[2:4],
            lat.at[0:2],
            halo_send.at[2],
            halo_recv.at[1],
            lax.rem(tm + 1, groups),
            tile,
        )

    def mix(first, second, third):
        even = first + third
        return first, even + second, even - second, third

    def mix_weights(k):
        for copy in part(k):
            copy.wait()
        column, first, count = PARTS[k]

        @pl.loop(0, count // STEP)
        def _(s):
            at_row = first + s * STEP
            by_row = []
            for a in range(3):
                rows = pl.ds(pl.multiple_of((3 * a + column) * C_MID + at_row, STEP), STEP)
                by_row.append(mix(*(w_mid[lag, rows, :].astype(F32) for lag in range(3))))
            rows = pl.ds(pl.multiple_of(column * C_MID + at_row, STEP), STEP)
            for i in range(4):
                by_time = mix(*(by_row[a][i] for a in range(3)))
                for r in range(4):
                    if (i, r) in MIXED:
                        u[MIXED.index((i, r)), rows, :] = by_time[r].astype(BF16)

    own.wait()
    spread_columns(cols, lat, 4, 2)
    @pl.when(tm == handed)
    def _():
        for k in range(2):
            mix_weights(k)

    expected = (
        len(row + column)
        + (tm < groups - 1).astype(jnp.int32)
        + jnp.logical_and(tm >= handed, tm < groups - 2).astype(jnp.int32)
        + jnp.logical_and(tm >= 1, tm <= relayed).astype(jnp.int32)
    )
    pl.semaphore_wait(barrier, expected)

    @pl.when(tm < groups - 1)
    def _():
        halo(1).start()

    @pl.when(jnp.logical_and(tm >= handed, tm < groups - 2))
    def _():
        halo(2).start()

    @pl.when(jnp.logical_and(tm >= 1, tm <= relayed))
    def _():
        pl.semaphore_signal(after, inc=1, device_id=(tm - 1, tile), device_id_type=MESH)

    tell(hop, column)

    @pl.when(tm != handed)
    def _():
        for k in range(2):
            mix_weights(k)

    @pl.when(tm == handed)
    def _():
        halo(1).wait_recv()
        hand_on().start()

    for k in range(2, 4):
        mix_weights(k)
    for copy in loads:
        copy.wait()

    @pl.when(tm < relayed)
    def _():
        pl.semaphore_wait(after, 1)
        halo(2).start()

    row = lax.broadcasted_iota(jnp.int32, (8, C_OUT), 0)
    head = w_head[...].astype(F32)
    by_color = jnp.where(
        row // 2 == 0,
        head[0:1],
        jnp.where(row // 2 == 1, head[1:2], jnp.where(row // 2 == 2, head[2:3], 0.0)),
    )
    head2 = jnp.concatenate(
        [jnp.where(row % 2 == 0, by_color, 0.0), jnp.where(row % 2 == 1, by_color, 0.0)], axis=1
    ).astype(BF16)

    weight = w_in[...].reshape(3 * TAPS, C_MID)

    def features(j):
        out = lax.dot_general(
            cols[j * TAPS : (j + 3) * TAPS, :],
            weight,
            (((0,), (0,)), ((), ())),
            preferred_element_type=F32,
        )
        out = (out + b_in[...]).astype(BF16)
        if j >= 2:
            by_pair = out.reshape(PAIRS, 2, TW, C_MID)
            for p in range(2):
                first_out[j - 2, p] = by_pair[:, p].reshape(HALF, C_MID)
        return silu(out.astype(F32))

    def keep(i, m):
        by_pair = m.reshape(PAIRS, 2, TW, C_MID)
        upper, lower = by_pair[:, 0], by_pair[:, 1]
        above = jnp.concatenate([upper[:1], lower[:-1]], axis=0)
        below = jnp.concatenate([upper[1:], lower[-1:]], axis=0)
        rows = (above - lower, 0.5 * (upper + lower), 0.5 * (lower - upper), upper - below)
        for r in range(4):
            v[4 * i + r] = rows[r].reshape(HALF, C_MID).astype(BF16)

    @pl.when(jnp.logical_and(tm >= 1, tm != handed))
    def _():
        halo(1).wait_recv()

    @pl.when(tm == 0)
    def _():
        for g in range(4):
            lat[g] = lat[4]

    spread_columns(cols, lat, 2, 2)
    act2 = features(2)
    act3 = features(3)
    for f in range(2):
        for p in range(2):
            base[f, p] = jnp.dot(first_out[f, p], w_skip[...], preferred_element_type=F32) + b_mid[...]

    @pl.when(tm >= 2)
    def _():
        halo(2).wait_recv()

    @pl.when(tm == 1)
    def _():
        for g in range(2):
            lat[g] = lat[2]

    spread_columns(cols, lat, 0, 2)
    act1 = features(1)
    keep(1, 0.5 * (act1 + act2))
    keep(2, 0.5 * (act2 - act1))
    keep(3, act1 - act3)
    keep(0, features(0) - act2)

    in_row = lax.broadcasted_iota(jnp.int32, (HALF, C_OUT), 0) % TW

    def product(i, r, e):
        if (i, r) in MIXED:
            weights = u[MIXED.index((i, r)), e * C_MID : (e + 1) * C_MID, :]
        else:
            tap = 6 + e if r else e
            weights = w_mid[2 if i else 0, tap * C_MID : (tap + 1) * C_MID, :]
        return jnp.dot(v[4 * i + r], weights, preferred_element_type=F32)

    def row_pair(i, e):
        for r in range(4):
            terms[i % 2, e, r] = product(i, r, e)
        p = [terms[i % 2, e, r] for r in range(4)]
        return p[0] + p[1] + p[2], p[1] - p[2] - p[3]

    def finish(f, p, sums):
        total = sums[1] + shift_rows(sums[0], in_row, -1) + shift_rows(sums[2], in_row, 1)
        total = silu(total + base[f, p]).astype(BF16)
        gated[:, p, :, f * C_OUT : (f + 1) * C_OUT] = total.reshape(PAIRS, TW, C_OUT)

    for e in range(3):
        first = row_pair(1, e)
        second = row_pair(2, e)
        for p in range(2):
            acc[0, p, e] = first[p] + second[p]
            acc[1, p, e] = first[p] - second[p]
    for f, i in ((0, 0), (1, 3)):
        last = [row_pair(i, e) for e in range(3)]
        for p in range(2):
            if f == 0:
                finish(f, p, [acc[f, p, e] + last[e][p] for e in range(3)])
            else:
                finish(f, p, [acc[f, p, e] - last[e][p] for e in range(3)])

    pixels = lax.dot_general(
        head2, gated[...].reshape(PIX, 2 * C_OUT), (((1,), (1,)), ((), ())), preferred_element_type=F32
    )
    pixels = pixels + jnp.where(
        row // 2 == 0, s_head_b[0], jnp.where(row // 2 == 1, s_head_b[1], s_head_b[2])
    )
    gather[tile] = jnp.concatenate([pixels[:, :128], pixels[:, 128:]], axis=0).astype(BF16)

    pl.semaphore_wait(hop, len(column))
    for dx, dy, dc in FAR_FIRST:
        to = at(x + dx, y + dy, core + dc)
        remote(gather.at[tile], gather.at[tile], all_send, all_recv, tm, to).start()
    everyone = remote(
        gather.at[0 : tiles - 1],
        gather.at[0 : tiles - 1],
        all_send,
        all_recv,
        tm,
        lax.rem(tile + 1, tiles),
    )

    found = jnp.int32(0)
    which = [jnp.int32(0)] * MAXLOAD
    taken = [jnp.int32(0)] * MAXLOAD
    for t in range(tiles):
        mine = s_writer[t] == tile
        for j in range(MAXLOAD):
            hit = jnp.logical_and(mine, found == j)
            which[j] = jnp.where(hit, t, which[j])
            taken[j] = jnp.where(hit, 1, taken[j])
        found = found + mine.astype(jnp.int32)

    everyone.wait_recv()

    def tile_pixels(t):
        block = gather[t].astype(F32)
        return jnp.concatenate([block[0:8], block[8:16]], axis=1)

    for j in range(MAXLOAD):
        live = jnp.full((8, PIX), taken[j], jnp.int32) > 0
        block = jnp.where(live, tile_pixels(which[j]), 0.0).astype(BF16)
        for c in range(3):
            written[j, c] = block[2 * c : 2 * c + 2]
    width = jnp.full((8, PIX), s_margin[0], jnp.int32)
    column = lax.broadcasted_iota(jnp.int32, (8, PIX), 1) % TW
    current = tile_pixels(tile)
    before = tile_pixels(jnp.maximum(tile - 1, 0))
    prior = pltpu.roll(before, PIX - TW + MARGIN_LO, 1)
    for m in range(MARGIN_LO + 1, MARGIN_HI + 1):
        prior = jnp.where(width == m, pltpu.roll(before, PIX - TW + m, 1), prior)
    fraction = column.astype(F32) / jnp.maximum(width, 1).astype(F32)
    mix = jnp.where(column < width, (1.0 - fraction) * prior + fraction * current, current)
    mix = mix.astype(BF16)
    for c in range(3):
        blended[0, c] = mix[2 * c : 2 * c + 2]
    everyone.wait_send()

    @pl.when(tm < groups - 1)
    def _():
        halo(1).wait_send()

    @pl.when(jnp.logical_and(tm != relayed, tm < groups - 2))
    def _():
        halo(2).wait_send()

    @pl.when(tm == handed)
    def _():
        hand_on().wait_send()


def copy_kernel(written_in, blended_in, written_out, blended_out, sem):
    copies = [
        pltpu.make_async_copy(written_in, written_out, sem.at[0]),
        pltpu.make_async_copy(blended_in, blended_out, sem.at[1]),
    ]
    for copy in copies:
        copy.start()
    for copy in copies:
        copy.wait()


def per_device(
    latents,
    writer,
    margin_cols,
    in_weight,
    in_bias,
    mid_weight,
    mid_bias,
    skip_weight,
    head_weight,
    head_bias,
):
    tiles = lax.axis_size("tile")
    groups = lax.axis_size("tm")
    frames = latents.shape[1]
    shapes = (
        jax.ShapeDtypeStruct((MAXLOAD, 3, frames, PIX), BF16),
        jax.ShapeDtypeStruct((1, 3, frames, PIX), BF16),
    )
    anywhere = pl.BlockSpec(memory_space=pl.ANY)

    def body(*refs):
        decode_kernel(tiles, groups, *refs)

    written, blended = pl.pallas_call(
        body,
        out_shape=tuple(pltpu.VMEM(s.shape, s.dtype) for s in shapes),
        in_specs=[anywhere] * 10,
        out_specs=(pl.BlockSpec(memory_space=pltpu.VMEM),) * 2,
        scratch_shapes=[
            pltpu.VMEM((6, C_LAT, PIX), BF16),
            pltpu.VMEM((6 * TAPS, PIX), BF16),
            pltpu.VMEM((3, TAPS, C_MID), BF16),
            pltpu.VMEM((1, C_MID), F32),
            pltpu.VMEM((3, 9 * C_MID, C_OUT), BF16),
            pltpu.VMEM((1, C_OUT), F32),
            pltpu.VMEM((C_MID, C_OUT), BF16),
            pltpu.VMEM((3, C_OUT), BF16),
            pltpu.VMEM((len(MIXED), 3 * C_MID, C_OUT), BF16),
            pltpu.VMEM((16, HALF, C_MID), BF16),
            pltpu.VMEM((2, 2, HALF, C_MID), BF16),
            pltpu.VMEM((2, 2, 3, HALF, C_OUT), F32),
            pltpu.VMEM((2, 2, HALF, C_OUT), F32),
            pltpu.VMEM((2, 3, 4, HALF, C_OUT), F32),
            pltpu.VMEM((PAIRS, 2, TW, 2 * C_OUT), BF16),
            pltpu.VMEM((tiles, 16, 128), BF16),
            pltpu.SMEM((tiles,), jnp.int32),
            pltpu.SMEM((1,), jnp.int32),
            pltpu.SMEM((3,), F32),
            pltpu.SemaphoreType.DMA((3,)),
            pltpu.SemaphoreType.DMA((2,)),
            pltpu.SemaphoreType.DMA,
            pltpu.SemaphoreType.DMA,
            pltpu.SemaphoreType.DMA((9,)),
            pltpu.SemaphoreType.DMA((36,)),
            pltpu.SemaphoreType.REGULAR,
            pltpu.SemaphoreType.REGULAR,
        ],
        compiler_params=pltpu.CompilerParams(
            collective_id=0, has_side_effects=True, vmem_limit_bytes=60 * 2**20
        ),
        name="decode",
    )(
        *(
            a if a is margin_cols else pltpu.with_memory_space_constraint(a, pltpu.HBM)
            for a in (
                latents,
                writer,
                margin_cols,
                in_weight,
                in_bias.reshape(1, -1),
                mid_weight,
                mid_bias.reshape(1, -1),
                skip_weight,
                head_weight.T,
                head_bias,
            )
        )
    )
    written, blended = pl.pallas_call(
        copy_kernel,
        out_shape=shapes,
        in_specs=[anywhere] * 2,
        out_specs=(anywhere,) * 2,
        scratch_shapes=[pltpu.SemaphoreType.DMA((2,))],
        name="hand_out",
    )(
        pltpu.with_memory_space_constraint(written, pltpu.VMEM),
        pltpu.with_memory_space_constraint(blended, pltpu.VMEM),
    )
    return written.transpose(0, 2, 1, 3), blended.transpose(0, 2, 1, 3)


def solution(mesh):
    return jax.shard_map(
        per_device,
        mesh=mesh,
        in_specs=(P("tile", "tm", None, None), P(), P("tile"), P(), P(), P(), P(), P(), P(), P()),
        out_specs=(P("tile", "tm", None, None), P("tile", "tm", None, None)),
        check_vma=False,
    )
```
